512 devices in a mesh: sample: 32 (over x_lo, y, core), feat: 16 (over z, x_hi).
Axes of the slice: x: 4 (x_hi: 2, x_lo: 2; x = x_hi * 2 + x_lo), y: 8, z: 8, core: 2. Of those that a mesh axis runs over, the one named last changes fastest.
Arguments:
- features: bfloat16 [131072, 4096], P('sample', 'feat'), may hold values from -6 to 6
- pre_one: bfloat16 [131072, 512], P(('sample', 'feat')), may hold values from -6 to 6
- pre_two: bfloat16 [131072, 512], P(('sample', 'feat')), may hold values from -6 to 6
- cotangent: bfloat16 [65536, 512], P(('sample', 'feat')), may hold values from -0.25 to 0.25
- weight_two: bfloat16 [512, 512], replicated, may hold values from -0.25 to 0.25
- weight_three: bfloat16 [512, 512], replicated, may hold values from -0.25 to 0.25
- lists_one: int32 [131072, 15], P('sample'), may hold values from 0 to 255
- degree_one: int32 [131072], P('sample'), may hold values from 1 to 15
- lists_two: int32 [131072, 10], P(('sample', 'feat')), may hold values from 0 to 255
- degree_two: int32 [131072], P(('sample', 'feat')), may hold values from 1 to 10
- lists_three: int32 [65536, 5], P(('sample', 'feat')), may hold values from 0 to 255
- degree_three: int32 [65536], P(('sample', 'feat')), may hold values from 1 to 5
Outputs:
- grad_one: float32 [4096, 512], P('feat')
- grad_two: float32 [512, 512], P('sample')
- grad_three: float32 [512, 512], P('sample')
The draws below stay inside these ranges and needn't reach their ends.
All inputs are finite; a program needn't handle non-finite values.
Results may differ from the reference program's by a relative error of at most 0.006.
Values may be sent and summed in bfloat16 or wider, within the bound.
No kernel may reach another device: no remote copies, remote signals or barrier semaphores. Data moves between devices by JAX's collectives and lax.ppermute only.
A program may use at most 64 MiB of HBM per device.

```python
import jax
import jax.numpy as jnp
from jax import lax

FEAT = 4096
HIDDEN_SIZE = 512
TGT = 128
FANOUT_ONE = 15
FANOUT_TWO = 10
FANOUT_THREE = 5
NODES = 256
BATCHES = 512
N_SAMPLE = 32
N_FEAT = 16
DEVICES = 512


def with_ends(values, rng, smallest, largest):
    place = [jax.random.randint(jax.random.fold_in(rng, axis), (), 0, length) for axis, length in enumerate(values.shape)]
    widest = values.shape.index(max(values.shape))
    neighbour = place[:widest] + [(place[widest] + 1) % values.shape[widest]] + place[widest + 1:]
    return values.at[tuple(place)].set(smallest).at[tuple(neighbour)].set(largest)


def with_spikes(drawn, own_key, source, target, shards_of, factor):
    owner, partner = [(jnp.arange(drawn.shape[dim]) // (drawn.shape[dim] // shards_of)).reshape([-1 if axis == dim else 1 for axis in range(drawn.ndim)]) for dim in (source, target)]
    chosen = jax.random.permutation(own_key, shards_of)[partner]
    strong = (owner == chosen) | (owner == (partner + shards_of // 2) % shards_of)
    return jnp.where(strong, factor * drawn, drawn)


def shard_levels(rng, shape, split, least, largest):
    factor_of = 1.0
    for position, shards_of in split:
        heights = jax.random.uniform(jax.random.fold_in(jax.random.fold_in(rng, 6), position), (shards_of,), jnp.float32, least / len(split), largest / len(split))
        factor_of = factor_of * jnp.repeat(jnp.exp(heights), shape[position] // shards_of).reshape((-1,) + (1,) * (len(shape) - 1 - position))
    return factor_of


def gaussian(key, extent, deviation, limit, split=(), kind=jnp.bfloat16):
    values = deviation * jax.random.normal(key, extent, jnp.float32)
    if split:
        values = values * shard_levels(key, extent, split, -0.22, 0.18)
    return jnp.clip(values, -limit, limit).astype(kind)


def heavy_noise(own_key, dims, scale, reach, pieces, heavy, kind=jnp.bfloat16):
    drawn = scale * jax.random.normal(own_key, dims, jnp.float32)
    if pieces:
        drawn = drawn * shard_levels(own_key, dims, pieces, -0.22, 0.18)
    return jnp.clip(with_spikes(drawn, jax.random.fold_in(own_key, 3), *heavy), -reach, reach).astype(kind)


def setup_inputs(seed: int = 0) -> dict:
    key_list = jax.random.split(jax.random.key(seed), 13)
    features = gaussian(key_list[0], (BATCHES * NODES, FEAT), 1.0, 6.0, ((0, 32), (1, 16)))
    pre_one = gaussian(key_list[1], (BATCHES * NODES, HIDDEN_SIZE), 1.0, 6.0, ((0, 512),))
    pre_two = gaussian(key_list[2], (BATCHES * NODES, HIDDEN_SIZE), 1.0, 6.0, ((0, 512),))
    cotangent = heavy_noise(key_list[3], (BATCHES * TGT, HIDDEN_SIZE), ((TGT * DEVICES) ** -0.5), 0.25, ((0, 512),), (0, 1, 512, 6.0))
    weight_two = gaussian(key_list[4], (HIDDEN_SIZE, HIDDEN_SIZE), HIDDEN_SIZE ** -0.5, 0.25)
    weight_three = gaussian(key_list[5], (HIDDEN_SIZE, HIDDEN_SIZE), HIDDEN_SIZE ** -0.5, 0.25)
    lists_one = with_ends(jax.random.randint(key_list[6], (BATCHES * NODES, FANOUT_ONE), 0, NODES), jax.random.fold_in(key_list[6], 1), 0, NODES - 1).astype(jnp.int32)
    degree_one = with_ends(jax.random.randint(key_list[7], (BATCHES * NODES,), 1, FANOUT_ONE + 1), jax.random.fold_in(key_list[7], 1), 1, FANOUT_ONE).astype(jnp.int32)
    lists_two = with_ends(jax.random.randint(key_list[8], (BATCHES * NODES, FANOUT_TWO), 0, NODES), jax.random.fold_in(key_list[8], 1), 0, NODES - 1).astype(jnp.int32)
    degree_two = with_ends(jax.random.randint(key_list[9], (BATCHES * NODES,), 1, FANOUT_TWO + 1), jax.random.fold_in(key_list[9], 1), 1, FANOUT_TWO).astype(jnp.int32)
    lists_three = with_ends(jax.random.randint(key_list[10], (BATCHES * TGT, FANOUT_THREE), 0, NODES), jax.random.fold_in(key_list[10], 1), 0, NODES - 1).astype(jnp.int32)
    degree_three = with_ends(jax.random.randint(key_list[11], (BATCHES * TGT,), 1, FANOUT_THREE + 1), jax.random.fold_in(key_list[11], 1), 1, FANOUT_THREE).astype(jnp.int32)
    return dict(features=features, pre_one=pre_one, pre_two=pre_two, cotangent=cotangent, weight_two=weight_two, weight_three=weight_three, lists_one=lists_one, degree_one=degree_one, lists_two=lists_two, degree_two=degree_two, lists_three=lists_three, degree_three=degree_three)


def count_tiles(neighbor_rows, degrees, width):
    columns = jnp.arange(width, dtype=jnp.int32)
    total = jnp.zeros((neighbor_rows.shape[0], width), jnp.float32)
    for column in range(neighbor_rows.shape[1]):
        hit = (neighbor_rows[:, column:column + 1] == columns[None, :]) & (column < degrees[:, None])
        total = total + hit.astype(jnp.float32)
    return total.astype(jnp.bfloat16)


def contract_rows(left, right):
    return lax.dot_general(left, right, (((0,), (0,)), ((), ())), preferred_element_type=jnp.float32)


def deep_layers(pre_one, pre_two, cotangent, weight_two, weight_three, lists_two, degree_two, lists_three, degree_three):
    hidden_two = jnp.maximum(pre_two, jnp.zeros_like(pre_two))
    hidden_one = jnp.maximum(pre_one, jnp.zeros_like(pre_one))
    tile_three = count_tiles(lists_three, degree_three, pre_two.shape[0])
    scale_three = degree_three.astype(jnp.float32)[:, None]
    mean_three = (jnp.dot(tile_three, hidden_two, preferred_element_type=jnp.float32) / scale_three).astype(jnp.bfloat16)
    term_three = contract_rows(mean_three, cotangent)
    back_three = (jnp.dot(cotangent, weight_three.T, preferred_element_type=jnp.float32) / scale_three).astype(jnp.bfloat16)
    delta_two = jnp.where(pre_two > 0, contract_rows(tile_three, back_three), 0.0).astype(jnp.bfloat16)
    tile_two = count_tiles(lists_two, degree_two, pre_one.shape[0])
    scale_two = degree_two.astype(jnp.float32)[:, None]
    mean_two = (jnp.dot(tile_two, hidden_one, preferred_element_type=jnp.float32) / scale_two).astype(jnp.bfloat16)
    term_two = contract_rows(mean_two, delta_two)
    back_two = (jnp.dot(delta_two, weight_two.T, preferred_element_type=jnp.float32) / scale_two).astype(jnp.bfloat16)
    delta_one = jnp.where(pre_one > 0, contract_rows(tile_two, back_two), 0.0).astype(jnp.bfloat16)
    return delta_one, term_two, term_three


def take_block(array, index, length):
    return lax.dynamic_slice_in_dim(array, (index * length).astype(jnp.int32), length, 0)


def reference(features, pre_one, pre_two, cotangent, weight_two, weight_three, lists_one, degree_one, lists_two, degree_two, lists_three, degree_three):
    def step(carry, index):
        acc_one, acc_two, acc_three = carry
        delta_one, term_two, term_three = deep_layers(
            take_block(pre_one, index, NODES), take_block(pre_two, index, NODES),
            take_block(cotangent, index, TGT), weight_two, weight_three,
            take_block(lists_two, index, NODES), take_block(degree_two, index, NODES),
            take_block(lists_three, index, TGT), take_block(degree_three, index, TGT))
        degrees = take_block(degree_one, index, NODES)
        tile_one = count_tiles(take_block(lists_one, index, NODES), degrees, NODES)
        summed = jnp.dot(tile_one, take_block(features, index, NODES), preferred_element_type=jnp.float32)
        mean_one = (summed / degrees.astype(jnp.float32)[:, None]).astype(jnp.bfloat16)
        acc_one = acc_one + contract_rows(mean_one, delta_one)
        return (acc_one, acc_two + term_two, acc_three + term_three), None

    start = (jnp.zeros((FEAT, HIDDEN_SIZE), jnp.float32), jnp.zeros((HIDDEN_SIZE, HIDDEN_SIZE), jnp.float32), jnp.zeros((HIDDEN_SIZE, HIDDEN_SIZE), jnp.float32))
    result, unused = lax.scan(step, start, jnp.arange(N_SAMPLE * N_FEAT, dtype=jnp.int32))
    return result[0], result[1], result[2]
```

```python
import jax
import jax.numpy as jnp
from jax import lax
from jax.sharding import Mesh, PartitionSpec as P

NODES = 256
AXES = ("xl", "y", "c", "z", "xh")
SAMPLE = ("xl", "y", "c")
FEAT = ("z", "xh")
Z = 8


def count_tiles(neighbor_rows, degrees, width):
    columns = jnp.arange(width, dtype=jnp.int32)
    total = jnp.zeros((neighbor_rows.shape[0], width), jnp.float32)
    for column in range(neighbor_rows.shape[1]):
        hit = (neighbor_rows[:, column : column + 1] == columns[None, :]) & (
            column < degrees[:, None]
        )
        total = total + hit.astype(jnp.float32)
    return total.astype(jnp.bfloat16)


def contract_rows(left, right):
    return lax.dot_general(
        left, right, (((0,), (0,)), ((), ())), preferred_element_type=jnp.float32
    )


def deep_layers(
    pre_one,
    pre_two,
    cotangent,
    weight_two,
    weight_three,
    lists_two,
    degree_two,
    lists_three,
    degree_three,
):
    hidden_two = jnp.maximum(pre_two, jnp.zeros_like(pre_two))
    hidden_one = jnp.maximum(pre_one, jnp.zeros_like(pre_one))
    tile_three = count_tiles(lists_three, degree_three, pre_two.shape[0])
    scale_three = degree_three.astype(jnp.float32)[:, None]
    mean_three = (
        jnp.dot(tile_three, hidden_two, preferred_element_type=jnp.float32) / scale_three
    ).astype(jnp.bfloat16)
    term_three = contract_rows(mean_three, cotangent)
    back_three = (
        jnp.dot(cotangent, weight_three.T, preferred_element_type=jnp.float32) / scale_three
    ).astype(jnp.bfloat16)
    delta_two = jnp.where(pre_two > 0, contract_rows(tile_three, back_three), 0.0).astype(
        jnp.bfloat16
    )
    tile_two = count_tiles(lists_two, degree_two, pre_one.shape[0])
    scale_two = degree_two.astype(jnp.float32)[:, None]
    mean_two = (
        jnp.dot(tile_two, hidden_one, preferred_element_type=jnp.float32) / scale_two
    ).astype(jnp.bfloat16)
    term_two = contract_rows(mean_two, delta_two)
    back_two = (
        jnp.dot(delta_two, weight_two.T, preferred_element_type=jnp.float32) / scale_two
    ).astype(jnp.bfloat16)
    delta_one = jnp.where(pre_one > 0, contract_rows(tile_two, back_two), 0.0).astype(jnp.bfloat16)
    return (delta_one, term_two, term_three)


def turn(block, sign):
    pairs = []
    for core in range(2):
        step = sign if core == 0 else -sign
        for z in range(Z):
            pairs.append((core * Z + z, core * Z + (z + step) % Z))
    return lax.ppermute(block, ("c", "z"), pairs)


def swap(block, axis):
    return lax.ppermute(block, axis, [(0, 1), (1, 0)])


def body(
    features,
    pre_one,
    pre_two,
    cotangent,
    weight_two,
    weight_three,
    lists_one,
    degree_one,
    lists_two,
    degree_two,
    lists_three,
    degree_three,
):
    bf = jnp.bfloat16
    f32 = jnp.float32
    z, xh, c = lax.axis_index("z"), lax.axis_index("xh"), lax.axis_index("c")
    width = features.shape[1]
    parts = features.reshape(Z, 2, NODES, width)

    def pick(array, index, axis):
        return lax.dynamic_index_in_dim(array, index, axis, keepdims=False)

    mine = pick(parts, xh, 1)
    theirs = swap(pick(parts, 1 - xh, 1), "xh")

    delta_one, term_two, term_three = deep_layers(
        pre_one,
        pre_two,
        cotangent,
        weight_two,
        weight_three,
        lists_two,
        degree_two,
        lists_three,
        degree_three,
    )
    own = z * 2 + xh
    own_lists = lax.dynamic_slice_in_dim(lists_one, own * NODES, NODES, 0)
    own_degree = lax.dynamic_slice_in_dim(degree_one, own * NODES, NODES, 0)
    tile_one = count_tiles(own_lists, own_degree, NODES)
    scaled = (delta_one.astype(f32) / own_degree.astype(f32)[:, None]).astype(bf)
    spread = contract_rows(tile_one, scaled).astype(bf)

    blocks = [(spread, z)]
    ahead = behind = spread
    sign = 1 - 2 * c
    for step in range(1, Z // 2 + 1):
        ahead = turn(ahead, 1)
        blocks.append((ahead, lax.rem(z - sign * step + Z, Z)))
        if step < Z // 2:
            behind = turn(behind, -1)
            blocks.append((behind, lax.rem(z + sign * step + Z, Z)))
    part_own = part_other = 0.0
    for block, index in blocks:
        part_own = part_own + contract_rows(pick(mine, index, 0), block)
        part_other = part_other + contract_rows(pick(theirs, index, 0), block)

    terms = jnp.stack([term_two, term_three]).reshape(2, 16, 2, 2, 8, 512)
    terms = pick(terms, c, 2) + swap(pick(terms, 1 - c, 2).astype(bf), "c").astype(f32)
    terms = terms.astype(bf).transpose(1, 2, 0, 3, 4)

    first = jnp.where(xh == 0, part_own, part_other)
    second = jnp.where(xh == 0, part_other, part_own)
    parted = jnp.stack([first, second]).reshape(2, 2, 128, 512)
    parted = pick(parted, c, 1) + swap(pick(parted, 1 - c, 1).astype(bf), "c").astype(f32)
    parted = parted.astype(bf).reshape(2, 16, 1, 8, 512).transpose(1, 0, 2, 3, 4)
    sent = jnp.concatenate([parted, terms], axis=2).reshape(32, 24, 512)
    got = lax.all_to_all(sent, ("xl", "y", "xh"), 0, 0)
    summed = jnp.sum(got.astype(f32), axis=0).astype(bf)

    def spread_out(piece, axes, count):
        return lax.all_to_all(jnp.broadcast_to(piece[None], (count,) + piece.shape), axes, 0, 0)

    half = spread_out(summed[:8], ("xl", "y"), 16).reshape(128, 512)
    other = swap(half, "c")
    low = jnp.where(c == 0, half, other)
    high = jnp.where(c == 0, other, half)
    grad_one = jnp.concatenate([low, high], axis=0).astype(f32)

    rest = spread_out(summed[8:], FEAT, 16).reshape(Z, 2, 2, 8, 512)
    rest = jnp.sum(rest.astype(f32), axis=0)
    grad_two = rest[:, 0].reshape(16, 512)
    grad_three = rest[:, 1].reshape(16, 512)
    return (grad_one, grad_two, grad_three)


def solution(mesh):
    fine = Mesh(mesh.devices.reshape(2, 8, 2, 8, 2), AXES)
    both = SAMPLE + FEAT
    return jax.shard_map(
        body,
        mesh=fine,
        in_specs=(
            P(SAMPLE, FEAT),
            P(both, None),
            P(both, None),
            P(both, None),
            P(),
            P(),
            P(SAMPLE, None),
            P(SAMPLE),
            P(both, None),
            P(both),
            P(both, None),
            P(both),
        ),
        out_specs=(P(FEAT, None), P(SAMPLE, None), P(SAMPLE, None)),
        check_vma=False,
    )
```

```python
import jax
import jax.numpy as jnp
from jax import lax
from jax.experimental import pallas as pl
from jax.experimental.pallas import tpu as pltpu
from jax.sharding import Mesh, PartitionSpec as P

NODES = 256
TGT = 128
HIDDEN = 512
AXES = ("xl", "y", "c", "z", "xh")
SAMPLE = ("xl", "y", "c")
FEAT = ("z", "xh")
Z = 8
BF = jnp.bfloat16
F32 = jnp.float32
MIB = 1024 * 1024


def mul(left, right, left_dim, right_dim):
    return lax.dot_general(
        left,
        right,
        (((left_dim,), (right_dim,)), ((), ())),
        preferred_element_type=F32,
    )


def tile_t(lists, degree):
    fan, rows = lists.shape
    nodes = lax.broadcasted_iota(jnp.int32, (NODES, rows), 0)
    total = jnp.zeros((NODES, rows), F32)
    for k in range(fan):
        valid = jnp.where(k < degree, lists[k : k + 1, :], -1)
        total = total + jnp.where(nodes == valid, 1.0, 0.0)
    return total.astype(BF)


def inverse_column(degree):
    rows = degree.shape[1]
    line = lax.broadcasted_iota(jnp.int32, (rows, rows), 0)
    column = lax.broadcasted_iota(jnp.int32, (rows, rows), 1)
    eye = jnp.where(line == column, 1.0, 0.0).astype(BF)
    spread = jnp.broadcast_to(degree.astype(F32), (128, rows)).astype(BF)
    return 1.0 / mul(eye, spread, 1, 1)


def scale_rows(values, inverse):
    return values * jnp.concatenate([inverse] * (values.shape[1] // 128), axis=1)


IN_VMEM = pl.BlockSpec(memory_space=pltpu.VMEM)
IN_HBM = pl.BlockSpec(memory_space=pltpu.HBM)
IN_SMEM = pl.BlockSpec(memory_space=pltpu.SMEM)


def call(kernel, name, out_shape, in_specs, scratch, flops, limit, operands):
    return pl.pallas_call(
        kernel,
        out_shape=out_shape,
        in_specs=in_specs,
        out_specs=tuple(IN_VMEM for unused in out_shape),
        scratch_shapes=scratch,
        compiler_params=pltpu.CompilerParams(vmem_limit_bytes=limit * MIB),
        cost_estimate=pl.CostEstimate(
            flops=flops, bytes_accessed=3_000_000, transcendentals=0
        ),
        name=name,
    )(*operands)


def chain_kernel(
    own,
    weight_three_hbm,
    cotangent_hbm,
    lists_three_hbm,
    degree_three_hbm,
    pre_two_hbm,
    lists_two_hbm,
    degree_two_hbm,
    weight_two_hbm,
    lists_one_hbm,
    degree_one_hbm,
    pre_one_hbm,
    spread_out,
    delta_out,
    tile_two_out,
    tile_three_out,
    weight_three,
    cotangent,
    lists_three,
    degree_three,
    pre_two,
    lists_two,
    degree_two,
    weight_two,
    lists_one,
    degree_one,
    pre_one,
    sems,
):
    columns = pl.ds(pl.multiple_of(own[0] * NODES, NODES), NODES)
    pairs = [
        (lists_three_hbm, lists_three),
        (degree_three_hbm, degree_three),
        (cotangent_hbm, cotangent),
        (weight_three_hbm, weight_three),
        (lists_two_hbm, lists_two),
        (degree_two_hbm, degree_two),
        (lists_one_hbm.at[:, columns], lists_one),
        (degree_one_hbm.at[:, columns], degree_one),
        (pre_two_hbm, pre_two),
        (weight_two_hbm, weight_two),
        (pre_one_hbm, pre_one),
    ]
    copies = [
        pltpu.make_async_copy(source, target, sems.at[index])
        for index, (source, target) in enumerate(pairs)
    ]
    for copy in copies:
        copy.start()
    for copy in copies[:2]:
        copy.wait()
    tile_three = tile_t(lists_three[...], degree_three[...])
    inverse_three = inverse_column(degree_three[...])
    tile_three_out[...] = tile_three
    for copy in copies[2:4]:
        copy.wait()
    back_three = scale_rows(mul(cotangent[...], weight_three[...], 1, 1), inverse_three)
    for copy in copies[4:8]:
        copy.wait()
    tile_two = tile_t(lists_two[...], degree_two[...])
    inverse_two = inverse_column(degree_two[...])
    tile_two_out[...] = tile_two
    tile_one = tile_t(lists_one[...], degree_one[...])
    inverse_one = inverse_column(degree_one[...])
    for copy in copies[8:]:
        copy.wait()
    up_two = mul(tile_three, back_three.astype(BF), 1, 0)
    delta_two = jnp.where(pre_two[...].astype(F32) > 0, up_two, 0.0).astype(BF)
    delta_out[...] = delta_two
    back_two = scale_rows(mul(delta_two, weight_two[...], 1, 1), inverse_two)
    up_one = mul(tile_two, back_two.astype(BF), 1, 0)
    delta_one = jnp.where(pre_one[...].astype(F32) > 0, up_one, 0.0).astype(BF)
    scaled = scale_rows(delta_one.astype(F32), inverse_one)
    high = scaled.astype(BF)
    low = (scaled - high.astype(F32)).astype(BF)
    spread = mul(tile_one, high, 1, 0) + mul(tile_one, low, 1, 0)
    spread_out[...] = spread.astype(BF)


def run_chain(own, arrays):
    shapes = [(array.shape, array.dtype) for array in arrays]
    for index in (8, 9):
        shapes[index] = ((shapes[index][0][0], NODES), shapes[index][1])
    return call(
        chain_kernel,
        "chain",
        (
            jax.ShapeDtypeStruct((NODES, HIDDEN), BF),
            jax.ShapeDtypeStruct((NODES, HIDDEN), BF),
            jax.ShapeDtypeStruct((NODES, NODES), BF),
            jax.ShapeDtypeStruct((NODES, TGT), BF),
        ),
        [IN_SMEM] + [IN_HBM] * len(arrays),
        [pltpu.VMEM(shape, kind) for shape, kind in shapes]
        + [pltpu.SemaphoreType.DMA((len(arrays),))],
        2 * 218_000_000,
        24,
        [own] + arrays,
    )


def terms_kernel(
    core,
    pre_one_hbm,
    pre_two_hbm,
    cotangent_hbm,
    degree_two_hbm,
    degree_three_hbm,
    delta_two,
    tile_two,
    tile_three,
    sent,
    kept,
    pre_one,
    pre_two,
    cotangent,
    degree_two,
    degree_three,
    total,
    sems,
):
    pairs = [
        (degree_three_hbm, degree_three),
        (pre_two_hbm, pre_two),
        (cotangent_hbm, cotangent),
        (degree_two_hbm, degree_two),
        (pre_one_hbm, pre_one),
    ]
    copies = [
        pltpu.make_async_copy(source, target, sems.at[index])
        for index, (source, target) in enumerate(pairs)
    ]
    for copy in copies:
        copy.start()
    for copy in copies:
        copy.wait()
    hidden_two = jnp.maximum(pre_two[...].astype(F32), 0.0).astype(BF)
    hidden_one = jnp.maximum(pre_one[...].astype(F32), 0.0).astype(BF)
    mean_three = scale_rows(
        mul(tile_three[...], hidden_two, 0, 0), inverse_column(degree_three[...])
    ).astype(BF)
    mean_two = scale_rows(
        mul(tile_two[...], hidden_one, 0, 0), inverse_column(degree_two[...])
    ).astype(BF)
    here = core[0]
    for which, (left, right) in enumerate(
        [(mean_two, delta_two[...]), (mean_three, cotangent[...])]
    ):
        total[...] = mul(left, right, 0, 0)
        for piece in range(16):
            mine = pl.multiple_of(piece * 32 + here * 16, 16)
            other = pl.multiple_of(piece * 32 + (1 - here) * 16, 16)
            kept[piece, which] = total[pl.ds(mine, 16), :]
            sent[piece, which] = total[pl.ds(other, 16), :].astype(BF)


def run_terms(core, inputs, inner):
    return call(
        terms_kernel,
        "terms",
        (
            jax.ShapeDtypeStruct((16, 2, 16, HIDDEN), BF),
            jax.ShapeDtypeStruct((16, 2, 16, HIDDEN), F32),
        ),
        [IN_SMEM] + [IN_HBM] * len(inputs) + [IN_VMEM] * len(inner),
        [pltpu.VMEM(array.shape, array.dtype) for array in inputs]
        + [
            pltpu.VMEM((HIDDEN, HIDDEN), F32),
            pltpu.SemaphoreType.DMA((len(inputs),)),
        ],
        2 * 151_000_000,
        24,
        [core] + inputs + inner,
    )


def run_fold(features, theirs, blocks, own_rows, other_rows, before):
    count, given = len(own_rows), len(blocks)
    width = features.shape[1]
    where = jnp.stack(list(own_rows) + list(other_rows)).astype(jnp.int32)
    start = [] if before is None else [before]
    extra = count > given

    def kernel(where, features_hbm, theirs_hbm, *refs):
        blocks, refs = refs[:given], refs[given:]
        start, refs = refs[: len(before_list)], refs[len(before_list) :]
        total, refs = refs[0], refs[1:]
        if extra:
            last, refs = refs[0], refs[1:]
        parts, sems = refs
        copies = []
        for side, source in enumerate((features_hbm, theirs_hbm)):
            for index in range(count):
                row = pl.multiple_of(where[side * count + index] * NODES, NODES)
                copy = pltpu.make_async_copy(
                    source.at[pl.ds(row, NODES), :],
                    parts.at[side, pl.ds(index * NODES, NODES), :],
                    sems.at[side, index],
                )
                copy.start()
                copies.append(copy)
        stacked = jnp.concatenate([block[...] for block in blocks], axis=0)
        for side in range(2):
            for copy in copies[side * count : side * count + given]:
                copy.wait()
            term = mul(parts[side, : given * NODES, :], stacked, 0, 0)
            total[side] = start[0][side] + term if start else term
        if extra:
            for side in range(2):
                copies[side * count + given].wait()
                last[side] = parts[side, given * NODES :, :].T

    before_list = start
    out_shape = (jax.ShapeDtypeStruct((2, width, HIDDEN), F32),)
    if extra:
        out_shape += (jax.ShapeDtypeStruct((2, width, NODES), BF),)
    return call(
        kernel,
        "fold",
        out_shape,
        [IN_SMEM, IN_HBM, IN_HBM] + [IN_VMEM] * (given + len(start)),
        [
            pltpu.VMEM((2, count * NODES, width), BF),
            pltpu.SemaphoreType.DMA((2, count)),
        ],
        given * 2 * 67_000_000,
        24,
        [where, features, theirs] + blocks + start,
    )


def run_last(total, last, block, core, half):
    width = total.shape[1]
    rows = width // 2
    where = jnp.stack([core, half]).astype(jnp.int32)

    def kernel(where, total, last, block, sent, kept, scratch):
        core, half = where[0], where[1]
        keep = pl.multiple_of(core * rows, rows)
        send = pl.multiple_of((1 - core) * rows, rows)
        for side in range(2):
            scratch[...] = total[side] + mul(last[side], block[...], 1, 0)
            place = half if side == 0 else 1 - half
            kept[place] = scratch[pl.ds(keep, rows), :]
            sent[place] = scratch[pl.ds(send, rows), :].astype(BF)

    return call(
        kernel,
        "last",
        (
            jax.ShapeDtypeStruct((2, rows, HIDDEN), BF),
            jax.ShapeDtypeStruct((2, rows, HIDDEN), F32),
        ),
        [IN_SMEM] + [IN_VMEM] * 3,
        [pltpu.VMEM((width, HIDDEN), F32)],
        2 * 70_000_000,
        16,
        [where, total, last, block],
    )


def turn(block, sign):
    pairs = []
    for core in range(2):
        step = sign if core == 0 else -sign
        for z in range(Z):
            pairs.append((core * Z + z, core * Z + (z + step) % Z))
    return lax.ppermute(block, ("c", "z"), pairs)


def swap(block, axis):
    return lax.ppermute(block, axis, [(0, 1), (1, 0)])


def after(*values):
    return lax.optimization_barrier(values)


def spread_out(piece, axes, count):
    return lax.all_to_all(jnp.broadcast_to(piece[None], (count,) + piece.shape), axes, 0, 0)


def body(
    features,
    pre_one,
    pre_two,
    cotangent,
    weight_two,
    weight_three,
    lists_one,
    degree_one,
    lists_two,
    degree_two,
    lists_three,
    degree_three,
):
    z, xh, c = lax.axis_index("z"), lax.axis_index("xh"), lax.axis_index("c")
    width = features.shape[1]

    own = jnp.reshape(z * 2 + xh, (1,)).astype(jnp.int32)
    core = jnp.reshape(c, (1,)).astype(jnp.int32)

    parts = features.reshape(Z, 2, NODES, width)
    give = lax.dynamic_index_in_dim(parts, 1 - xh, 1, keepdims=False)
    own, give = after(own, give)
    theirs = swap(give, "xh").reshape(Z * NODES, width)

    lists = [lists_one.T, lists_two.T, lists_three.T]
    degrees = [degree_one[None], degree_two[None], degree_three[None]]
    spread, delta_two, tile_two, tile_three = run_chain(
        own,
        [weight_three, cotangent, lists[2], degrees[2], pre_two, lists[1], degrees[1]]
        + [weight_two, lists[0], degrees[0], pre_one],
    )

    ahead, behind = [spread], [spread]

    def step_on():
        ahead.append(turn(ahead[-1], 1))
        if len(behind) < Z // 2:
            behind.append(turn(behind[-1], -1))

    step_on()
    sent, kept = run_terms(
        core,
        [pre_one, pre_two, cotangent, degrees[1], degrees[2]],
        [delta_two, tile_two, tile_three],
    )
    ahead[1], behind[1], sent = after(ahead[1], behind[1], sent)
    step_on()
    other = swap(sent, "c")
    ahead[2], behind[2], other = after(ahead[2], behind[2], other)
    step_on()
    terms = (kept + other.astype(F32)).astype(BF).reshape(32, 16, HIDDEN)
    terms = lax.all_to_all(terms, ("xl", "y", "xh"), 0, 0)
    ahead[3], behind[3] = after(ahead[3], behind[3])
    step_on()

    sign = 1 - 2 * c

    def places(steps):
        rows = [lax.rem(z + sign * step + Z, Z) for step in steps]
        return [row * 2 + xh for row in rows], rows

    (total,) = run_fold(
        features, theirs, [spread, behind[1], ahead[1], behind[2], ahead[2]],
        *places([0, 1, -1, 2, -2]), None
    )
    total, last = run_fold(
        features, theirs, [behind[3], ahead[3]], *places([3, -3, -4]), total
    )
    sent, kept = run_last(total, last, ahead[4], c, xh)
    total = (kept + swap(sent, "c").astype(F32)).astype(BF).reshape(32, 8, HIDDEN)
    total = lax.all_to_all(total, ("xh", "xl", "y"), 0, 0)

    def double(terms, step):
        return terms + lax.ppermute(terms, "z", [(k, k ^ step) for k in range(Z)])

    terms = jnp.sum(terms.astype(F32), axis=0)
    terms = double(double(terms, 1), 2)
    total, terms = after(total, terms)
    total = jnp.sum(total.astype(F32), axis=0).astype(BF)
    total = spread_out(total, ("xl", "y"), 16).reshape(width // 2, HIDDEN)
    terms = double(terms, 4)
    other = swap(terms, "xh")
    total, terms, other = after(total, terms, other)
    grad_one = lax.all_gather(total, "c", axis=0, tiled=True).astype(F32)
    grad_two = jnp.where(xh == 0, terms, other)
    grad_three = jnp.where(xh == 0, other, terms)
    return (grad_one, grad_two, grad_three)


def solution(mesh):
    fine = Mesh(mesh.devices.reshape(2, 8, 2, 8, 2), AXES)
    both = SAMPLE + FEAT
    return jax.shard_map(
        body,
        mesh=fine,
        in_specs=(
            P(SAMPLE, FEAT),
            P(both, None),
            P(both, None),
            P(both, None),
            P(),
            P(),
            P(SAMPLE, None),
            P(SAMPLE),
            P(both, None),
            P(both),
            P(both, None),
            P(both),
        ),
        out_specs=(P(FEAT, None), P(SAMPLE, None), P(SAMPLE, None)),
        check_vma=False,
    )
```

```python
import jax
import jax.numpy as jnp
from jax import lax
from jax.experimental import pallas as pl
from jax.experimental.pallas import tpu as pltpu
from jax.sharding import Mesh, PartitionSpec as P

NODES = 256
TGT = 128
HIDDEN = 512
AXES = ("xl", "y", "c", "z", "xh")
SAMPLE = ("xl", "y", "c")
FEAT = ("z", "xh")
Z = 8
BF = jnp.bfloat16
F32 = jnp.float32
MIB = 1024 * 1024


def mul(left, right, left_dim, right_dim):
    return lax.dot_general(
        left,
        right,
        (((left_dim,), (right_dim,)), ((), ())),
        preferred_element_type=F32,
    )


def tile_t(lists, degree):
    fan, rows = lists.shape
    nodes = lax.broadcasted_iota(jnp.int32, (NODES, rows), 0)
    total = jnp.zeros((NODES, rows), F32)
    for k in range(fan):
        valid = jnp.where(k < degree, lists[k : k + 1, :], -1)
        total = total + jnp.where(nodes == valid, 1.0, 0.0)
    return total.astype(BF)


def inverse_column(degree):
    rows = degree.shape[1]
    line = lax.broadcasted_iota(jnp.int32, (rows, rows), 0)
    column = lax.broadcasted_iota(jnp.int32, (rows, rows), 1)
    eye = jnp.where(line == column, 1.0, 0.0).astype(BF)
    spread = jnp.broadcast_to(degree.astype(F32), (128, rows)).astype(BF)
    return 1.0 / mul(eye, spread, 1, 1)


def scale_rows(values, inverse):
    return values * jnp.concatenate([inverse] * (values.shape[1] // 128), axis=1)


IN_VMEM = pl.BlockSpec(memory_space=pltpu.VMEM)
IN_HBM = pl.BlockSpec(memory_space=pltpu.HBM)
IN_SMEM = pl.BlockSpec(memory_space=pltpu.SMEM)


def call(kernel, name, out_shape, in_specs, scratch, flops, limit, operands):
    return pl.pallas_call(
        kernel,
        out_shape=out_shape,
        in_specs=in_specs,
        out_specs=tuple(IN_VMEM for unused in out_shape),
        scratch_shapes=scratch,
        compiler_params=pltpu.CompilerParams(vmem_limit_bytes=limit * MIB),
        cost_estimate=pl.CostEstimate(
            flops=flops, bytes_accessed=3_000_000, transcendentals=0
        ),
        name=name,
    )(*operands)


def chain_kernel(
    own,
    weight_three_hbm,
    cotangent_hbm,
    lists_three_hbm,
    degree_three_hbm,
    pre_two_hbm,
    lists_two_hbm,
    degree_two_hbm,
    weight_two_hbm,
    lists_one_hbm,
    degree_one_hbm,
    pre_one_hbm,
    spread_out,
    delta_out,
    tile_two_out,
    tile_three_out,
    weight_three,
    cotangent,
    lists_three,
    degree_three,
    pre_two,
    lists_two,
    degree_two,
    weight_two,
    lists_one,
    degree_one,
    pre_one,
    sems,
):
    columns = pl.ds(pl.multiple_of(own[0] * NODES, NODES), NODES)
    pairs = [
        (lists_three_hbm, lists_three),
        (degree_three_hbm, degree_three),
        (cotangent_hbm, cotangent),
        (weight_three_hbm, weight_three),
        (lists_two_hbm, lists_two),
        (degree_two_hbm, degree_two),
        (lists_one_hbm.at[:, columns], lists_one),
        (degree_one_hbm.at[:, columns], degree_one),
        (pre_two_hbm, pre_two),
        (weight_two_hbm, weight_two),
        (pre_one_hbm, pre_one),
    ]
    copies = [
        pltpu.make_async_copy(source, target, sems.at[index])
        for index, (source, target) in enumerate(pairs)
    ]
    for copy in copies:
        copy.start()
    for copy in copies[:2]:
        copy.wait()
    tile_three = tile_t(lists_three[...], degree_three[...])
    inverse_three = inverse_column(degree_three[...])
    tile_three_out[...] = tile_three
    for copy in copies[2:4]:
        copy.wait()
    back_three = scale_rows(mul(cotangent[...], weight_three[...], 1, 1), inverse_three)
    for copy in copies[4:8]:
        copy.wait()
    tile_two = tile_t(lists_two[...], degree_two[...])
    inverse_two = inverse_column(degree_two[...])
    tile_two_out[...] = tile_two
    tile_one = tile_t(lists_one[...], degree_one[...])
    inverse_one = inverse_column(degree_one[...])
    for copy in copies[8:]:
        copy.wait()
    up_two = mul(tile_three, back_three.astype(BF), 1, 0)
    delta_two = jnp.where(pre_two[...].astype(F32) > 0, up_two, 0.0).astype(BF)
    delta_out[...] = delta_two
    back_two = scale_rows(mul(delta_two, weight_two[...], 1, 1), inverse_two)
    up_one = mul(tile_two, back_two.astype(BF), 1, 0)
    delta_one = jnp.where(pre_one[...].astype(F32) > 0, up_one, 0.0).astype(BF)
    scaled = scale_rows(delta_one.astype(F32), inverse_one)
    high = scaled.astype(BF)
    low = (scaled - high.astype(F32)).astype(BF)
    spread = mul(tile_one, high, 1, 0) + mul(tile_one, low, 1, 0)
    spread_out[...] = spread.astype(BF)


def run_chain(own, arrays):
    shapes = [(array.shape, array.dtype) for array in arrays]
    for index in (8, 9):
        shapes[index] = ((shapes[index][0][0], NODES), shapes[index][1])
    return call(
        chain_kernel,
        "chain",
        (
            jax.ShapeDtypeStruct((NODES, HIDDEN), BF),
            jax.ShapeDtypeStruct((NODES, HIDDEN), BF),
            jax.ShapeDtypeStruct((NODES, NODES), BF),
            jax.ShapeDtypeStruct((NODES, TGT), BF),
        ),
        [IN_SMEM] + [IN_HBM] * len(arrays),
        [pltpu.VMEM(shape, kind) for shape, kind in shapes]
        + [pltpu.SemaphoreType.DMA((len(arrays),))],
        2 * 218_000_000,
        24,
        [own] + arrays,
    )


def terms_kernel(
    core,
    pre_one_hbm,
    pre_two_hbm,
    cotangent_hbm,
    degree_two_hbm,
    degree_three_hbm,
    delta_two,
    tile_two,
    tile_three,
    sent,
    kept,
    pre_one,
    pre_two,
    cotangent,
    degree_two,
    degree_three,
    total,
    sems,
):
    pairs = [
        (degree_three_hbm, degree_three),
        (pre_two_hbm, pre_two),
        (cotangent_hbm, cotangent),
        (degree_two_hbm, degree_two),
        (pre_one_hbm, pre_one),
    ]
    copies = [
        pltpu.make_async_copy(source, target, sems.at[index])
        for index, (source, target) in enumerate(pairs)
    ]
    for copy in copies:
        copy.start()
    for copy in copies:
        copy.wait()
    hidden_two = jnp.maximum(pre_two[...].astype(F32), 0.0).astype(BF)
    hidden_one = jnp.maximum(pre_one[...].astype(F32), 0.0).astype(BF)
    mean_three = scale_rows(
        mul(tile_three[...], hidden_two, 0, 0), inverse_column(degree_three[...])
    ).astype(BF)
    mean_two = scale_rows(
        mul(tile_two[...], hidden_one, 0, 0), inverse_column(degree_two[...])
    ).astype(BF)
    here = core[0]
    for which, (left, right) in enumerate(
        [(mean_two, delta_two[...]), (mean_three, cotangent[...])]
    ):
        total[...] = mul(left, right, 0, 0)
        for piece in range(16):
            mine = pl.multiple_of(piece * 32 + here * 16, 16)
            other = pl.multiple_of(piece * 32 + (1 - here) * 16, 16)
            kept[piece, which] = total[pl.ds(mine, 16), :]
            sent[piece, which] = total[pl.ds(other, 16), :].astype(BF)


def run_terms(core, inputs, inner):
    return call(
        terms_kernel,
        "terms",
        (
            jax.ShapeDtypeStruct((16, 2, 16, HIDDEN), BF),
            jax.ShapeDtypeStruct((16, 2, 16, HIDDEN), F32),
        ),
        [IN_SMEM] + [IN_HBM] * len(inputs) + [IN_VMEM] * len(inner),
        [pltpu.VMEM(array.shape, array.dtype) for array in inputs]
        + [
            pltpu.VMEM((HIDDEN, HIDDEN), F32),
            pltpu.SemaphoreType.DMA((len(inputs),)),
        ],
        2 * 151_000_000,
        24,
        [core] + inputs + inner,
    )


def run_fold(features, theirs, blocks, own_rows, other_rows, before):
    count, given = len(own_rows), len(blocks)
    width = features.shape[1]
    where = jnp.stack(list(own_rows) + list(other_rows)).astype(jnp.int32)
    start = [] if before is None else [before]
    extra = count > given

    def kernel(where, features_hbm, theirs_hbm, *refs):
        blocks, refs = refs[:given], refs[given:]
        start, refs = refs[: len(before_list)], refs[len(before_list) :]
        total, refs = refs[0], refs[1:]
        if extra:
            last, refs = refs[0], refs[1:]
        parts, sems = refs
        copies = []
        for side, source in enumerate((features_hbm, theirs_hbm)):
            for index in range(count):
                row = pl.multiple_of(where[side * count + index] * NODES, NODES)
                copy = pltpu.make_async_copy(
                    source.at[pl.ds(row, NODES), :],
                    parts.at[side, pl.ds(index * NODES, NODES), :],
                    sems.at[side, index],
                )
                copy.start()
                copies.append(copy)
        stacked = jnp.concatenate([block[...] for block in blocks], axis=0)
        for side in range(2):
            for copy in copies[side * count : side * count + given]:
                copy.wait()
            term = mul(parts[side, : given * NODES, :], stacked, 0, 0)
            total[side] = start[0][side] + term if start else term
        if extra:
            for side in range(2):
                copies[side * count + given].wait()
                last[side] = parts[side, given * NODES :, :].T

    before_list = start
    out_shape = (jax.ShapeDtypeStruct((2, width, HIDDEN), F32),)
    if extra:
        out_shape += (jax.ShapeDtypeStruct((2, width, NODES), BF),)
    return call(
        kernel,
        "fold",
        out_shape,
        [IN_SMEM, IN_HBM, IN_HBM] + [IN_VMEM] * (given + len(start)),
        [
            pltpu.VMEM((2, count * NODES, width), BF),
            pltpu.SemaphoreType.DMA((2, count)),
        ],
        given * 2 * 67_000_000,
        24,
        [where, features, theirs] + blocks + start,
    )


def run_last(total, last, block, half):
    where = jnp.reshape(half, (1,)).astype(jnp.int32)

    def kernel(where, total, last, block, sent):
        for side in range(2):
            place = where[0] if side == 0 else 1 - where[0]
            sent[place] = (total[side] + mul(last[side], block[...], 1, 0)).astype(BF)

    return call(
        kernel,
        "last",
        (jax.ShapeDtypeStruct(total.shape, BF),),
        [IN_SMEM] + [IN_VMEM] * 3,
        [],
        2 * 70_000_000,
        16,
        [where, total, last, block],
    )[0]


def turn(block, sign):
    pairs = []
    for core in range(2):
        step = sign if core == 0 else -sign
        for z in range(Z):
            pairs.append((core * Z + z, core * Z + (z + step) % Z))
    return lax.ppermute(block, ("c", "z"), pairs)


def swap(block, axis):
    return lax.ppermute(block, axis, [(0, 1), (1, 0)])


def after(*values):
    return lax.optimization_barrier(values)


def spread_out(piece, axes, count):
    return lax.all_to_all(jnp.broadcast_to(piece[None], (count,) + piece.shape), axes, 0, 0)


def body(
    features,
    pre_one,
    pre_two,
    cotangent,
    weight_two,
    weight_three,
    lists_one,
    degree_one,
    lists_two,
    degree_two,
    lists_three,
    degree_three,
):
    z, xh, c = lax.axis_index("z"), lax.axis_index("xh"), lax.axis_index("c")
    width = features.shape[1]

    own = jnp.reshape(z * 2 + xh, (1,)).astype(jnp.int32)
    core = jnp.reshape(c, (1,)).astype(jnp.int32)

    parts = features.reshape(Z, 2, NODES, width)
    give = lax.dynamic_index_in_dim(parts, 1 - xh, 1, keepdims=False)
    own, give = after(own, give)
    theirs = swap(give, "xh").reshape(Z * NODES, width)

    lists = [lists_one.T, lists_two.T, lists_three.T]
    degrees = [degree_one[None], degree_two[None], degree_three[None]]
    spread, delta_two, tile_two, tile_three = run_chain(
        own,
        [weight_three, cotangent, lists[2], degrees[2], pre_two, lists[1], degrees[1]]
        + [weight_two, lists[0], degrees[0], pre_one],
    )

    ahead, behind = [spread], [spread]

    def step_on():
        ahead.append(turn(ahead[-1], 1))
        if len(behind) < Z // 2:
            behind.append(turn(behind[-1], -1))

    step_on()
    sent, kept = run_terms(
        core,
        [pre_one, pre_two, cotangent, degrees[1], degrees[2]],
        [delta_two, tile_two, tile_three],
    )
    ahead[1], behind[1], sent = after(ahead[1], behind[1], sent)
    step_on()
    other = swap(sent, "c")
    ahead[2], behind[2], other = after(ahead[2], behind[2], other)
    step_on()
    terms = (kept + other.astype(F32)).astype(BF).reshape(32, 16, HIDDEN)
    terms = lax.all_to_all(terms, ("xl", "y", "xh"), 0, 0)
    ahead[3], behind[3] = after(ahead[3], behind[3])
    step_on()

    sign = 1 - 2 * c

    def places(steps):
        rows = [lax.rem(z + sign * step + Z, Z) for step in steps]
        return [row * 2 + xh for row in rows], rows

    (total,) = run_fold(
        features, theirs, [spread, behind[1], ahead[1], behind[2], ahead[2]],
        *places([0, 1, -1, 2, -2]), None
    )
    total, last = run_fold(
        features, theirs, [behind[3], ahead[3]], *places([3, -3, -4]), total
    )
    total = run_last(total, last, ahead[4], xh).reshape(64, 8, HIDDEN)
    total = lax.all_to_all(total, ("xh", "c", "xl", "y"), 0, 0)

    def double(terms, step):
        return terms + lax.ppermute(terms, "z", [(k, k ^ step) for k in range(Z)])

    terms = jnp.sum(terms.astype(F32), axis=0)
    terms = double(double(terms, 1), 2)
    total, terms = after(total, terms)
    total = jnp.sum(total.astype(F32), axis=0).astype(BF)
    total = spread_out(total, ("c", "xl", "y"), 32).reshape(width, HIDDEN)
    terms = double(terms, 4)
    other = swap(terms, "xh")
    grad_one = total.astype(F32)
    grad_two = jnp.where(xh == 0, terms, other)
    grad_three = jnp.where(xh == 0, other, terms)
    return (grad_one, grad_two, grad_three)


def solution(mesh):
    fine = Mesh(mesh.devices.reshape(2, 8, 2, 8, 2), AXES)
    both = SAMPLE + FEAT
    return jax.shard_map(
        body,
        mesh=fine,
        in_specs=(
            P(SAMPLE, FEAT),
            P(both, None),
            P(both, None),
            P(both, None),
            P(),
            P(),
            P(SAMPLE, None),
            P(SAMPLE),
            P(both, None),
            P(both),
            P(both, None),
            P(both),
        ),
        out_specs=(P(FEAT, None), P(SAMPLE, None), P(SAMPLE, None)),
        check_vma=False,
    )
```
